32 devices in a mesh: wide: 8 (over y, x, core), narrow: 4 (over z).
Axes of the slice: x: 2, y: 2, z: 4, core: 2. Of those that a mesh axis runs over, the one named last changes fastest.
Arguments:
- currents: float32 [2, 2, 1024, 8192], P(None, None, 'wide', 'narrow'), may hold values from -6 to 6
- far_gradient: float32 [2, 2, 1024, 1024], P(None, None, 'wide', 'narrow'), may hold values from -24 to 24
Outputs:
- far_field: float32 [2, 2, 1024, 1024], P(None, None, 'wide', 'narrow')
- aperture_grad: float32 [2, 2, 1024, 8192], P(None, None, 'wide', 'narrow')
The draws below stay inside these ranges and needn't reach their ends.
All inputs are finite; a program needn't handle non-finite values.
Results may differ from the reference program's by a relative error of at most 0.0001.
Values sent between devices are 32-bit elements; how exact they have to be, the bound alone decides.
No kernel may reach another device: no remote copies, remote signals or barrier semaphores. Data moves between devices by JAX's collectives and lax.ppermute only.
A program may use at most 128 MiB of HBM per device.

```python
import math
import jax
import jax.numpy as jnp
from jax import lax

NX = 8192
MX = 1024
MY = 1024
STRIDE = 4
NY = 1024


def block_scale(stream_key, extent, split, low, high):
    def one(axis_at, shards_of):
        draws = jax.random.uniform(jax.random.fold_in(jax.random.fold_in(stream_key, 6), axis_at), (shards_of,), jnp.float32, low / len(split), high / len(split))
        return jnp.repeat(jnp.exp(draws), extent[axis_at] // shards_of).reshape((-1,) + (1,) * (len(extent) - axis_at - 1))

    factor_of = one(*split[0])
    for cut in split[1:]:
        factor_of = factor_of * one(*cut)
    return factor_of


def bell_draw(key, shape, scale, most, pieces=(), kind=jnp.bfloat16):
    values = jax.random.normal(key, shape, jnp.float32) * scale
    if len(pieces) > 0:
        values = block_scale(key, shape, pieces, -0.22, 0.18) * values
    return jnp.clip(values, min=-most, max=most).astype(kind)


def setup_inputs(seed: int = 0) -> dict:
    keys = jax.random.split(jax.random.key(seed), 3)
    return {
        "currents": bell_draw(keys[0], (2, 2, NY, NX), 1.0, 6.0, ((2, 8), (3, 4)), jnp.float32),
        "far_gradient": bell_draw(keys[1], (2, 2, MY, MX), 4.0, 24.0, ((2, 8), (3, 4)), jnp.float32),
    }


precise = lax.Precision.HIGHEST

def phase_table(pos_start, pos_count, pos_total, ang_count, modulus):
    position = pos_start + jnp.arange(pos_count, dtype=jnp.int32) - pos_total // 2
    angles = jnp.arange(ang_count, dtype=jnp.int32) - ang_count // 2
    cycles = jnp.mod(position[:, None] * angles[None, :] * STRIDE, modulus)
    radians = 2.0 * math.pi / modulus * cycles.astype(jnp.float32)
    return (jnp.cos(radians), jnp.sin(radians))

def matmul(left, right):
    return jnp.dot(left, right, precision=precise, preferred_element_type=jnp.float32)

def reference(currents, far_gradient):
    cos_x, sin_x = phase_table(0, NX, NX, MX, NX)
    cos_y, sin_y = phase_table(0, NY, NY, MY, NX)
    scale = 1.0 / math.sqrt(NY * NX)
    far_parts = []
    grad_parts = []
    for component in range(2):
        real_cur = currents[component, 0]
        imag_cur = currents[component, 1]
        sum_real = matmul(real_cur, cos_x) + matmul(imag_cur, sin_x)
        sum_imag = matmul(imag_cur, cos_x) - matmul(real_cur, sin_x)
        far_real = scale * (matmul(cos_y.T, sum_real) + matmul(sin_y.T, sum_imag))
        far_imag = scale * (matmul(cos_y.T, sum_imag) - matmul(sin_y.T, sum_real))
        far_parts.append(jnp.stack([far_real, far_imag]))
        grad_real = far_gradient[component, 0]
        grad_imag = far_gradient[component, 1]
        half_real = matmul(grad_real, cos_x.T) - matmul(grad_imag, sin_x.T)
        half_imag = matmul(grad_imag, cos_x.T) + matmul(grad_real, sin_x.T)
        back_real = scale * (matmul(cos_y, half_real) - matmul(sin_y, half_imag))
        back_imag = scale * (matmul(cos_y, half_imag) + matmul(sin_y, half_real))
        grad_parts.append(jnp.stack([back_real, back_imag]))
    return (jnp.stack(far_parts), jnp.stack(grad_parts))
```

```python
import functools
import math

import jax
import jax.numpy as jnp
import numpy as np
from jax import lax
from jax.experimental import pallas as pl
from jax.experimental.pallas import tpu as pltpu
from jax.sharding import PartitionSpec as P

NX = 8192
MX = 1024
MY = 1024
STRIDE = 4

PERIOD = NX // STRIDE
RADIX = 4
SPAN = PERIOD // RADIX
BANDS = MX // RADIX
LANES = 128
HALF = LANES // 2

f32 = jnp.float32
bf16 = jnp.bfloat16
precise = lax.Precision.HIGHEST


def phase_table(pos_start, pos_count, pos_total, ang_count, modulus):
    position = pos_start + jnp.arange(pos_count, dtype=jnp.int32) - pos_total // 2
    angles = jnp.arange(ang_count, dtype=jnp.int32) - ang_count // 2
    cycles = jnp.mod(position[:, None] * angles[None, :] * STRIDE, modulus)
    radians = 2.0 * math.pi / modulus * cycles.astype(jnp.float32)
    return (jnp.cos(radians), jnp.sin(radians))


def contract(left, right, left_dim, right_dim):
    return lax.dot_general(
        left,
        right,
        (((left_dim,), (right_dim,)), ((), ())),
        precision=precise,
        preferred_element_type=jnp.float32,
    )


def general_body(currents, far_gradient):
    row_count = currents.shape[2]
    column_count = currents.shape[3]
    angle_rows = far_gradient.shape[2]
    angle_cols = far_gradient.shape[3]
    total_rows = row_count * lax.axis_size("wide")
    scale = 1.0 / math.sqrt(total_rows * NX)
    row_start = lax.axis_index("wide") * row_count
    column_start = lax.axis_index("narrow") * column_count
    cos_x, sin_x = phase_table(column_start, column_count, NX, MX, NX)
    cos_y, sin_y = phase_table(row_start, row_count, total_rows, MY, NX)
    real_cur = currents[:, 0].reshape(2 * row_count, column_count)
    imag_cur = currents[:, 1].reshape(2 * row_count, column_count)
    real_term = contract(cos_x, real_cur, 0, 1) + contract(sin_x, imag_cur, 0, 1)
    imag_term = contract(cos_x, imag_cur, 0, 1) - contract(sin_x, real_cur, 0, 1)
    column_sums = lax.psum_scatter(
        jnp.stack([real_term, imag_term], axis=1), "narrow", scatter_dimension=0, tiled=True
    )
    sum_real = column_sums[:, 0].reshape(angle_cols * 2, row_count)
    sum_imag = column_sums[:, 1].reshape(angle_cols * 2, row_count)
    real_term = contract(cos_y, sum_real, 0, 1) + contract(sin_y, sum_imag, 0, 1)
    imag_term = contract(cos_y, sum_imag, 0, 1) - contract(sin_y, sum_real, 0, 1)
    far_sums = lax.psum_scatter(
        scale * jnp.stack([real_term, imag_term], axis=1), "wide", scatter_dimension=0, tiled=True
    )
    far_field = far_sums.reshape(angle_rows, 2, angle_cols, 2).transpose(3, 1, 0, 2)
    grad_real = far_gradient[:, 0].transpose(1, 2, 0).reshape(angle_rows, angle_cols * 2)
    grad_imag = far_gradient[:, 1].transpose(1, 2, 0).reshape(angle_rows, angle_cols * 2)
    piece_real = lax.all_gather(grad_real, "wide", axis=0, tiled=True)
    piece_imag = lax.all_gather(grad_imag, "wide", axis=0, tiled=True)
    half_real = contract(piece_real, cos_y, 0, 1) - contract(piece_imag, sin_y, 0, 1)
    half_imag = contract(piece_imag, cos_y, 0, 1) + contract(piece_real, sin_y, 0, 1)
    half_real = half_real.reshape(angle_cols, 2, row_count)
    half_imag = half_imag.reshape(angle_cols, 2, row_count)
    piece_real = lax.all_gather(half_real, "narrow", axis=0, tiled=True)
    piece_imag = lax.all_gather(half_imag, "narrow", axis=0, tiled=True)
    width = piece_real.shape[0]
    flat_real = piece_real.reshape(width, 2 * row_count)
    flat_imag = piece_imag.reshape(width, 2 * row_count)
    back_real = contract(flat_real, cos_x, 0, 1) - contract(flat_imag, sin_x, 0, 1)
    back_imag = contract(flat_imag, cos_x, 0, 1) + contract(flat_real, sin_x, 0, 1)
    back_real = back_real.reshape(2, row_count, column_count)
    back_imag = back_imag.reshape(2, row_count, column_count)
    aperture_grad = scale * jnp.stack([back_real, back_imag], axis=1)
    return (far_field, aperture_grad)


def halves(table):
    hi = table.astype(np.float32).astype(bf16)
    return hi, (table - hi.astype(np.float64)).astype(np.float32).astype(bf16)


def angle(count_left, left_start, count_right, right_start, period):
    left = np.arange(count_left, dtype=np.int64) + left_start
    right = np.arange(count_right, dtype=np.int64) + right_start
    return 2.0 * np.pi / period * ((left[:, None] * right[None, :]) % period)


def make_tables(shards):
    theta = angle(SPAN, 0, BANDS, -(BANDS // 2), SPAN)
    cos, sin = np.cos(theta), np.sin(theta)
    each = BANDS // shards
    x_table = np.zeros((2, SPAN, shards, 2, each))
    x_table[0, :, :, 0] = cos.reshape(SPAN, shards, each)
    x_table[1, :, :, 0] = sin.reshape(SPAN, shards, each)
    x_table[0, :, :, 1] = -sin.reshape(SPAN, shards, each)
    x_table[1, :, :, 1] = cos.reshape(SPAN, shards, each)
    x_table = x_table.reshape(2 * SPAN, 2 * BANDS)
    y_table = np.concatenate([cos.T, sin.T], axis=0)
    y_back = np.concatenate([cos, sin], axis=0)
    twiddle = angle(RADIX, 0, SPAN, 0, PERIOD)
    cols = RADIX * each
    order = np.zeros((2, cols, RADIX, 2, each))
    for k0 in range(RADIX):
        for j in range(each):
            for part in range(2):
                order[part, RADIX * j + k0, k0, part, j] = 1.0
    order = order.reshape(2 * cols, 2 * cols).astype(bf16)
    return {
        "x": halves(x_table),
        "x_back": halves(np.ascontiguousarray(x_table.T)),
        "y": halves(y_table),
        "y_back": halves(y_back),
        "row_tw": np.concatenate([np.cos(twiddle), np.sin(twiddle)], axis=0).astype(np.float32),
        "col_tw": np.ascontiguousarray(
            np.concatenate([np.cos(twiddle), np.sin(twiddle)], axis=0).T
        ).astype(np.float32),
        "order": order,
        "order_back": np.ascontiguousarray(order.T),
    }


def split(value):
    hi = value.astype(bf16)
    return hi, (value - hi.astype(f32)).astype(bf16)


def dot(left, right):
    return jnp.dot(left, right, preferred_element_type=f32)


def dot3(left, right_hi, right_lo):
    hi, lo = split(left)
    return dot(hi, right_hi) + (dot(lo, right_hi) + dot(hi, right_lo))


def times(tw_cos, tw_sin, real, imag):
    return real * tw_cos + imag * tw_sin, imag * tw_cos - real * tw_sin


def x_kernel(cur, tw, t_hi, t_lo, out):
    rows = cur.shape[2]
    re = [cur[0, 0, :, a * SPAN : (a + 1) * SPAN] for a in range(RADIX)]
    im = [cur[0, 1, :, a * SPAN : (a + 1) * SPAN] for a in range(RADIX)]
    sum_re, dif_re = re[0] + re[2], re[0] - re[2]
    sum_im, dif_im = im[0] + im[2], im[0] - im[2]
    odd_re, gap_re = re[1] + re[3], re[1] - re[3]
    odd_im, gap_im = im[1] + im[3], im[1] - im[3]
    legs = [
        (sum_re + odd_re, sum_im + odd_im),
        (dif_re + gap_im, dif_im - gap_re),
        (sum_re - odd_re, sum_im - odd_im),
        (dif_re - gap_im, dif_im + gap_re),
    ]
    flat = []
    for k0, (real, imag) in enumerate(legs):
        if k0 > 0:
            real, imag = times(tw[k0 : k0 + 1], tw[RADIX + k0 : RADIX + k0 + 1], real, imag)
        flat.append(jnp.concatenate([real, imag], axis=1))
    sums = dot3(jnp.concatenate(flat, axis=0), t_hi[...], t_lo[...])
    for shard in range(out.shape[0]):
        for k0 in range(RADIX):
            out[shard, k0] = sums[k0 * rows : (k0 + 1) * rows, shard * LANES : (shard + 1) * LANES]


def sign_of(shape):
    lane = lax.broadcasted_iota(jnp.int32, shape, len(shape) - 1)
    return jnp.where(lane < HALF, 1.0, -1.0).astype(f32)


def swap(value):
    return pltpu.roll(value, HALF, axis=1)


def y_kernel(scale, col, tw, t_hi, t_lo, out):
    early, late = col[:SPAN], col[SPAN:]
    sign = sign_of(early.shape)
    turned = sign * swap(early)
    flat = []
    for k0, leg in enumerate([late + early, late - turned, late - early, late + turned]):
        if k0 > 0:
            leg = leg * tw[:, k0 : k0 + 1] + (sign * tw[:, RADIX + k0 : RADIX + k0 + 1]) * swap(leg)
        flat.append(leg)
    hi, lo = split(jnp.concatenate(flat, axis=1))
    both = dot(t_hi[...], hi) + (dot(t_hi[...], lo) + dot(t_lo[...], hi))
    half_sign = scale * sign_of((BANDS, LANES))
    for k0 in range(RADIX):
        cos_part = both[:BANDS, k0 * LANES : (k0 + 1) * LANES]
        sin_part = both[BANDS:, k0 * LANES : (k0 + 1) * LANES]
        out[pl.ds(k0, BANDS, stride=RADIX), :] = scale * cos_part + half_sign * swap(sin_part)


def y_back_kernel(scale, grad, tw, t_hi, t_lo, out):
    flat = [grad[pl.ds(k0, BANDS, stride=RADIX), :] for k0 in range(RADIX)]
    hi, lo = split(jnp.concatenate(flat, axis=1))
    both = dot(t_hi[...], hi) + (dot(t_hi[...], lo) + dot(t_lo[...], hi))
    sign = sign_of((SPAN, LANES))
    legs = []
    for k0 in range(RADIX):
        cos_part = both[:SPAN, k0 * LANES : (k0 + 1) * LANES]
        sin_part = both[SPAN:, k0 * LANES : (k0 + 1) * LANES]
        leg = cos_part - sign * swap(sin_part)
        if k0 > 0:
            leg = leg * tw[:, k0 : k0 + 1] - (sign * tw[:, RADIX + k0 : RADIX + k0 + 1]) * swap(leg)
        legs.append(leg)
    even, odd = legs[0] + legs[2], legs[1] + legs[3]
    out[SPAN:, :] = scale * (even + odd)
    out[:SPAN, :] = scale * ((legs[0] - legs[2]) + sign * swap(legs[1] - legs[3]))


def x_back_kernel(shards, place, *refs):
    own, rights, lefts = refs[0], refs[1:shards], refs[shards : 2 * shards - 1]
    tw, t_hi, t_lo, _, out, hi_ref, lo_ref = refs[2 * shards - 1 :]
    rows = own.shape[1]
    me = place[0]
    for step in range(shards):
        block = own[...] if step == 0 else lefts[step - 1][...] + rights[shards - 1 - step][...]
        hi, lo = split(block.reshape(RADIX * rows, LANES))
        at = pl.ds(pl.multiple_of(lax.rem(me + step, shards) * LANES, LANES), LANES)
        hi_ref[:, at] = hi
        lo_ref[:, at] = lo
    hi, lo = hi_ref[...], lo_ref[...]
    sums = dot(hi, t_hi[...]) + (dot(lo, t_hi[...]) + dot(hi, t_lo[...]))
    legs = []
    for k0 in range(RADIX):
        real = sums[k0 * rows : (k0 + 1) * rows, :SPAN]
        imag = sums[k0 * rows : (k0 + 1) * rows, SPAN:]
        if k0 > 0:
            real, imag = times(tw[k0 : k0 + 1], -tw[RADIX + k0 : RADIX + k0 + 1], real, imag)
        legs.append((real, imag))
    (r0, i0), (r1, i1), (r2, i2), (r3, i3) = legs
    even_r, even_i, gap_r, gap_i = r0 + r2, i0 + i2, r0 - r2, i0 - i2
    odd_r, odd_i, skew_r, skew_i = r1 + r3, i1 + i3, r1 - r3, i1 - i3
    results = [
        (even_r + odd_r, even_i + odd_i),
        (gap_r - skew_i, gap_i + skew_r),
        (even_r - odd_r, even_i - odd_i),
        (gap_r + skew_i, gap_i - skew_r),
    ]
    for a, (real, imag) in enumerate(results):
        out[0, 0, :, a * SPAN : (a + 1) * SPAN] = real
        out[0, 1, :, a * SPAN : (a + 1) * SPAN] = imag


def moved(value, order):
    hi = value.astype(bf16)
    rest = value - hi.astype(f32)
    mid = rest.astype(bf16)
    lo = (rest - mid.astype(f32)).astype(bf16)
    return dot(hi, order) + (dot(mid, order) + dot(lo, order))


def sort_kernel(grad, order, out):
    for component in range(2):
        flat = jnp.concatenate([grad[component, 0], grad[component, 1]], axis=1)
        sorted_ = moved(flat, order[...])
        for k0 in range(RADIX):
            out[component * RADIX + k0] = sorted_[:, k0 * LANES : (k0 + 1) * LANES]


def unsort_kernel(blocks, order, out):
    cols = out.shape[3]
    for component in range(2):
        flat = jnp.concatenate([blocks[component * RADIX + k0] for k0 in range(RADIX)], axis=1)
        far = moved(flat, order[...])
        out[component, 0] = far[:, :cols]
        out[component, 1] = far[:, cols:]


PARAMS = pltpu.CompilerParams(vmem_limit_bytes=40 * 1024 * 1024)


def cost(macs, nbytes):
    return pl.CostEstimate(flops=2 * macs, bytes_accessed=nbytes, transcendentals=0)


def whole(kernel, shape, *args, macs=1 << 28):
    return pl.pallas_call(
        kernel,
        out_shape=jax.ShapeDtypeStruct(shape, f32),
        in_specs=[pl.BlockSpec(memory_space=pltpu.VMEM)] * len(args),
        out_specs=pl.BlockSpec(memory_space=pltpu.VMEM),
        compiler_params=PARAMS,
        cost_estimate=cost(macs, 1 << 22),
    )(*args)


def fixed(shape):
    return pl.BlockSpec(shape, lambda *_: (0,) * len(shape))


def project_x(currents, component, shards, tables):
    rows, columns = currents.shape[2:]
    tile = rows // 2
    t_hi, t_lo = tables["x"]
    return pl.pallas_call(
        x_kernel,
        grid=(rows // tile,),
        out_shape=jax.ShapeDtypeStruct((shards, RADIX, rows, LANES), f32),
        in_specs=[
            pl.BlockSpec((1, 2, tile, columns), lambda i: (component, 0, i, 0)),
            fixed((2 * RADIX, SPAN)),
            fixed(t_hi.shape),
            fixed(t_lo.shape),
        ],
        out_specs=pl.BlockSpec((shards, RADIX, tile, LANES), lambda i: (0, 0, i, 0)),
        compiler_params=PARAMS,
        cost_estimate=cost(RADIX * rows * 3 * t_hi.size, 8 << 20),
    )(currents, tables["row_tw"], t_hi, t_lo)


def back_x(place, parts, component, grad, shape, tables):
    shards = (len(parts) + 1) // 2
    rows = shape[2]
    tile = rows // 2
    t_hi, t_lo = tables["x_back"]
    block = pl.BlockSpec((RADIX, tile, LANES), lambda i, _: (0, i, 0))
    first = grad is None
    kernel = functools.partial(x_back_kernel, shards)
    if first:
        grad = tables["row_tw"]
    return pl.pallas_call(
        kernel,
        grid_spec=pltpu.PrefetchScalarGridSpec(
            num_scalar_prefetch=1,
            grid=(rows // tile,),
            in_specs=[block] * len(parts)
            + [
                fixed((2 * RADIX, SPAN)),
                fixed(t_hi.shape),
                fixed(t_lo.shape),
                pl.BlockSpec(memory_space=pl.ANY),
            ],
            out_specs=pl.BlockSpec((1, 2, tile, shape[3]), lambda i, _: (component, 0, i, 0)),
            scratch_shapes=[
                pltpu.VMEM((RADIX * tile, 2 * BANDS), bf16),
                pltpu.VMEM((RADIX * tile, 2 * BANDS), bf16),
            ],
        ),
        out_shape=jax.ShapeDtypeStruct(shape, f32),
        input_output_aliases={} if first else {1 + len(parts) + 3: 0},
        compiler_params=PARAMS,
        cost_estimate=cost(RADIX * rows * 3 * t_hi.size, 8 << 20),
    )(place, *parts, tables["row_tw"], t_hi, t_lo, grad)


def line_sum(blocks, shards):
    me = lax.axis_index("narrow")

    def pick(index):
        return lax.dynamic_index_in_dim(blocks, jnp.clip(index, 0, shards - 1), 0, False)

    right = left = None
    for step in range(shards - 1):
        to_right = pick(me + shards - 1 - step)
        to_left = pick(me - (shards - 1 - step))
        if step > 0:
            to_right, to_left = to_right + right, to_left + left
        right = lax.ppermute(to_right, "narrow", [(i, i + 1) for i in range(step + 1)])
        left = lax.ppermute(
            to_left, "narrow", [(shards - 1 - i, shards - 2 - i) for i in range(step + 1)]
        )
    return pick(me) + (right + left)


def line_gather(block, shards):
    rights, lefts = [], []
    right = left = block
    for step in range(shards - 1):
        right = lax.ppermute(right, "narrow", [(i, i + 1) for i in range(step, shards - 1)])
        left = lax.ppermute(left, "narrow", [(i + 1, i) for i in range(shards - 1 - step)])
        rights.append(right)
        lefts.append(left)
    return [block, *rights, *lefts]


def fast_body(tables, currents, far_gradient):
    shards = lax.axis_size("narrow")
    wide = lax.axis_size("wide")
    rows = currents.shape[2]
    angle_rows = far_gradient.shape[2]
    scale = 1.0 / math.sqrt(rows * wide * NX)
    place = lax.axis_index("narrow").astype(jnp.int32).reshape(1)
    y_hi, y_lo = tables["y"]
    b_hi, b_lo = tables["y_back"]

    sums = [project_x(currents, c, shards, tables) for c in range(2)]
    sorted_ = whole(sort_kernel, (2 * RADIX, angle_rows, LANES), far_gradient, tables["order"])

    rows_in = lax.all_to_all(sorted_, "wide", 0, 0).reshape(MY, LANES)
    rows_out = whole(
        functools.partial(y_back_kernel, scale), (rows * wide, LANES), rows_in, tables["col_tw"], b_hi, b_lo
    )
    half = lax.all_to_all(rows_out.reshape(wide, rows, LANES), "wide", 0, 0)

    columns = jnp.concatenate([line_sum(s, shards) for s in sums], axis=0)
    rows_in = lax.all_to_all(columns, "wide", 0, 0).reshape(rows * wide, LANES)
    rows_out = whole(
        functools.partial(y_kernel, scale), (MY, LANES), rows_in, tables["col_tw"], y_hi, y_lo
    )
    far = lax.all_to_all(rows_out.reshape(wide, angle_rows, LANES), "wide", 0, 0)
    far_field = whole(unsort_kernel, far_gradient.shape, far, tables["order_back"])

    grad = None
    for c in range(2):
        parts = line_gather(half[c * RADIX : (c + 1) * RADIX], shards)
        grad = back_x(place, parts, c, grad, currents.shape, tables)
    return (far_field, grad)


def solution(mesh):
    spec = P(None, None, "wide", "narrow")
    shards, wide = mesh.shape["narrow"], mesh.shape["wide"]

    def run(currents, far_gradient):
        rows = currents.shape[2]
        fits = (
            currents.shape[3] == shards * PERIOD
            and rows == 2 * SPAN
            and far_gradient.shape[2] == MY == 2 * SPAN
            and BANDS // shards == HALF
            and wide == 2 * RADIX
        )
        body = functools.partial(fast_body, make_tables(shards)) if fits else general_body
        return jax.shard_map(
            body, mesh=mesh, in_specs=(spec, spec), out_specs=(spec, spec), check_vma=False
        )(currents, far_gradient)

    return run
```

```python
import functools
import math

import jax
import jax.numpy as jnp
import numpy as np
from jax import lax
from jax.experimental import pallas as pl
from jax.experimental.pallas import tpu as pltpu
from jax.sharding import PartitionSpec as P

NX = 8192
MX = 1024
MY = 1024
STRIDE = 4

PERIOD = NX // STRIDE
RADIX = 4
SPAN = PERIOD // RADIX
BANDS = MX // RADIX
LANES = 128
HALF = LANES // 2

f32 = jnp.float32
bf16 = jnp.bfloat16
precise = lax.Precision.HIGHEST


def phase_table(pos_start, pos_count, pos_total, ang_count, modulus):
    position = pos_start + jnp.arange(pos_count, dtype=jnp.int32) - pos_total // 2
    angles = jnp.arange(ang_count, dtype=jnp.int32) - ang_count // 2
    cycles = jnp.mod(position[:, None] * angles[None, :] * STRIDE, modulus)
    radians = 2.0 * math.pi / modulus * cycles.astype(jnp.float32)
    return (jnp.cos(radians), jnp.sin(radians))


def contract(left, right, left_dim, right_dim):
    return lax.dot_general(
        left,
        right,
        (((left_dim,), (right_dim,)), ((), ())),
        precision=precise,
        preferred_element_type=jnp.float32,
    )


def general_body(currents, far_gradient):
    row_count = currents.shape[2]
    column_count = currents.shape[3]
    angle_rows = far_gradient.shape[2]
    angle_cols = far_gradient.shape[3]
    total_rows = row_count * lax.axis_size("wide")
    scale = 1.0 / math.sqrt(total_rows * NX)
    row_start = lax.axis_index("wide") * row_count
    column_start = lax.axis_index("narrow") * column_count
    cos_x, sin_x = phase_table(column_start, column_count, NX, MX, NX)
    cos_y, sin_y = phase_table(row_start, row_count, total_rows, MY, NX)
    real_cur = currents[:, 0].reshape(2 * row_count, column_count)
    imag_cur = currents[:, 1].reshape(2 * row_count, column_count)
    real_term = contract(cos_x, real_cur, 0, 1) + contract(sin_x, imag_cur, 0, 1)
    imag_term = contract(cos_x, imag_cur, 0, 1) - contract(sin_x, real_cur, 0, 1)
    column_sums = lax.psum_scatter(
        jnp.stack([real_term, imag_term], axis=1), "narrow", scatter_dimension=0, tiled=True
    )
    sum_real = column_sums[:, 0].reshape(angle_cols * 2, row_count)
    sum_imag = column_sums[:, 1].reshape(angle_cols * 2, row_count)
    real_term = contract(cos_y, sum_real, 0, 1) + contract(sin_y, sum_imag, 0, 1)
    imag_term = contract(cos_y, sum_imag, 0, 1) - contract(sin_y, sum_real, 0, 1)
    far_sums = lax.psum_scatter(
        scale * jnp.stack([real_term, imag_term], axis=1), "wide", scatter_dimension=0, tiled=True
    )
    far_field = far_sums.reshape(angle_rows, 2, angle_cols, 2).transpose(3, 1, 0, 2)
    grad_real = far_gradient[:, 0].transpose(1, 2, 0).reshape(angle_rows, angle_cols * 2)
    grad_imag = far_gradient[:, 1].transpose(1, 2, 0).reshape(angle_rows, angle_cols * 2)
    piece_real = lax.all_gather(grad_real, "wide", axis=0, tiled=True)
    piece_imag = lax.all_gather(grad_imag, "wide", axis=0, tiled=True)
    half_real = contract(piece_real, cos_y, 0, 1) - contract(piece_imag, sin_y, 0, 1)
    half_imag = contract(piece_imag, cos_y, 0, 1) + contract(piece_real, sin_y, 0, 1)
    half_real = half_real.reshape(angle_cols, 2, row_count)
    half_imag = half_imag.reshape(angle_cols, 2, row_count)
    piece_real = lax.all_gather(half_real, "narrow", axis=0, tiled=True)
    piece_imag = lax.all_gather(half_imag, "narrow", axis=0, tiled=True)
    width = piece_real.shape[0]
    flat_real = piece_real.reshape(width, 2 * row_count)
    flat_imag = piece_imag.reshape(width, 2 * row_count)
    back_real = contract(flat_real, cos_x, 0, 1) - contract(flat_imag, sin_x, 0, 1)
    back_imag = contract(flat_imag, cos_x, 0, 1) + contract(flat_real, sin_x, 0, 1)
    back_real = back_real.reshape(2, row_count, column_count)
    back_imag = back_imag.reshape(2, row_count, column_count)
    aperture_grad = scale * jnp.stack([back_real, back_imag], axis=1)
    return (far_field, aperture_grad)


def halves(table):
    hi = table.astype(np.float32).astype(bf16)
    return hi, (table - hi.astype(np.float64)).astype(np.float32).astype(bf16)


def angle(count_left, left_start, count_right, right_start, period):
    left = np.arange(count_left, dtype=np.int64) + left_start
    right = np.arange(count_right, dtype=np.int64) + right_start
    return 2.0 * np.pi / period * ((left[:, None] * right[None, :]) % period)


def make_tables(shards):
    theta = angle(SPAN, 0, BANDS, -(BANDS // 2), SPAN)
    cos, sin = np.cos(theta), np.sin(theta)
    each = BANDS // shards
    x_table = np.stack([cos.reshape(SPAN, shards, each), -sin.reshape(SPAN, shards, each)], axis=2)
    x_table = x_table.reshape(SPAN, 2 * BANDS)
    y_table = np.concatenate([cos.T, sin.T], axis=0)
    y_back = np.concatenate([cos, sin], axis=0)
    twiddle = angle(RADIX, 0, SPAN, 0, PERIOD)
    cols = RADIX * each
    order = np.zeros((each, RADIX, RADIX, each))
    for k0 in range(RADIX):
        order[np.arange(each), k0, k0, np.arange(each)] = 1.0
    order = order.reshape(cols, cols).astype(bf16)
    return {
        "x": halves(x_table),
        "x_back": halves(np.ascontiguousarray(x_table.T)),
        "y": halves(y_table),
        "y_back": halves(y_back),
        "row_tw": np.concatenate([np.cos(twiddle), np.sin(twiddle)], axis=0).astype(np.float32),
        "col_tw": np.ascontiguousarray(
            np.concatenate([np.cos(twiddle), np.sin(twiddle)], axis=0).T
        ).astype(np.float32),
        "order": order,
        "order_back": np.ascontiguousarray(order.T),
    }


def split(value):
    hi = value.astype(bf16)
    return hi, (value - hi.astype(f32)).astype(bf16)


def dot(left, right):
    return jnp.dot(left, right, preferred_element_type=f32)


def dot3(left, right):
    return dot(left[0], right[0]) + (dot(left[1], right[0]) + dot(left[0], right[1]))


def times(tw_cos, tw_sin, real, imag):
    return real * tw_cos + imag * tw_sin, imag * tw_cos - real * tw_sin


def sign_of(shape):
    lane = lax.broadcasted_iota(jnp.int32, shape, len(shape) - 1)
    return jnp.where(lane < HALF, 1.0, -1.0).astype(f32)


def swap(value):
    return pltpu.roll(value, HALF, axis=1)


def moved(value, order):
    hi = value.astype(bf16)
    rest = value - hi.astype(f32)
    mid = rest.astype(bf16)
    lo = (rest - mid.astype(f32)).astype(bf16)
    return dot(hi, order) + (dot(mid, order) + dot(lo, order))


def paired(first, second):
    left = lax.broadcasted_iota(jnp.int32, first.shape, 1) < HALF
    return jnp.where(left, first, swap(second)), jnp.where(left, swap(first), second)


def sort(grad, order, out):
    rows = grad.shape[2]
    for component in range(2):
        flat = jnp.concatenate([grad[component, 0], grad[component, 1]], axis=0)
        places = moved(flat, order[...])
        for pair in range(RADIX // 2):
            lanes = places[:, pair * LANES : (pair + 1) * LANES]
            at = component * RADIX + 2 * pair
            out[at], out[at + 1] = paired(lanes[:rows], lanes[rows:])


def start_kernel(shards, place, cur, tw, t_hi, t_lo, grad, order, sorted_, *refs):
    outs, held = refs[:-1], refs[-1]
    rows = cur.shape[2]

    @pl.when((pl.program_id(0) == 0) & (pl.program_id(1) == 0))
    def _():
        sort(grad, order, sorted_)

    re = [cur[0, 0, :, a * SPAN : (a + 1) * SPAN] for a in range(RADIX)]
    im = [cur[0, 1, :, a * SPAN : (a + 1) * SPAN] for a in range(RADIX)]
    sum_re, dif_re = re[0] + re[2], re[0] - re[2]
    sum_im, dif_im = im[0] + im[2], im[0] - im[2]
    odd_re, gap_re = re[1] + re[3], re[1] - re[3]
    odd_im, gap_im = im[1] + im[3], im[1] - im[3]
    legs = [
        (sum_re + odd_re, sum_im + odd_im),
        (dif_re + gap_im, dif_im - gap_re),
        (sum_re - odd_re, sum_im - odd_im),
        (dif_re - gap_im, dif_im + gap_re),
    ]
    flat = []
    for k0, (real, imag) in enumerate(legs):
        if k0 > 0:
            real, imag = times(tw[k0 : k0 + 1], tw[RADIX + k0 : RADIX + k0 + 1], real, imag)
        flat += [real, imag]
    sums = dot3(split(jnp.concatenate(flat, axis=0)), (t_hi[...], t_lo[...]))
    sign = sign_of((rows, LANES))
    for shard in range(shards):
        lanes = sums[:, shard * LANES : (shard + 1) * LANES]
        for k0 in range(RADIX):
            of_real = lanes[2 * k0 * rows : (2 * k0 + 1) * rows]
            of_imag = lanes[(2 * k0 + 1) * rows : (2 * k0 + 2) * rows]
            held[shard, k0] = of_real - sign * swap(of_imag)
    for away, out in enumerate(outs):
        out[...] = held[place[0] ^ away]


def y_kernel(scale, col, tw, t_hi, t_lo, *refs):
    out = refs[-1]
    early, late = col[:SPAN], col[SPAN:]
    sign = sign_of(early.shape)
    turned = sign * swap(early)
    flat = []
    for k0, leg in enumerate([late + early, late - turned, late - early, late + turned]):
        if k0 > 0:
            leg = leg * tw[:, k0 : k0 + 1] + (sign * tw[:, RADIX + k0 : RADIX + k0 + 1]) * swap(leg)
        flat.append(leg)
    hi, lo = split(jnp.concatenate(flat, axis=1))
    both = dot3((t_hi[...], t_lo[...]), (hi, lo))
    half_sign = scale * sign_of((BANDS, LANES))
    for k0 in range(RADIX):
        cos_part = both[:BANDS, k0 * LANES : (k0 + 1) * LANES]
        sin_part = both[BANDS:, k0 * LANES : (k0 + 1) * LANES]
        out[pl.ds(k0, BANDS, stride=RADIX), :] = scale * cos_part + half_sign * swap(sin_part)


def y_back_kernel(scale, grad, tw, t_hi, t_lo, *refs):
    out = refs[-1]
    flat = [grad[pl.ds(k0, BANDS, stride=RADIX), :] for k0 in range(RADIX)]
    hi, lo = split(jnp.concatenate(flat, axis=1))
    both = dot3((t_hi[...], t_lo[...]), (hi, lo))
    sign = sign_of((SPAN, LANES))
    legs = []
    for k0 in range(RADIX):
        cos_part = both[:SPAN, k0 * LANES : (k0 + 1) * LANES]
        sin_part = both[SPAN:, k0 * LANES : (k0 + 1) * LANES]
        leg = cos_part - sign * swap(sin_part)
        if k0 > 0:
            leg = leg * tw[:, k0 : k0 + 1] - (sign * tw[:, RADIX + k0 : RADIX + k0 + 1]) * swap(leg)
        legs.append(leg)
    even, odd = legs[0] + legs[2], legs[1] + legs[3]
    out[SPAN:, :] = scale * (even + odd)
    out[:SPAN, :] = scale * ((legs[0] - legs[2]) + sign * swap(legs[1] - legs[3]))


def x_back_kernel(place, _, *refs):
    blocks, (tw, t_hi, t_lo, out, hi_ref, lo_ref) = refs[:-6], refs[-6:]
    rows = out.shape[2]
    flat = RADIX * rows
    sign = sign_of((flat, LANES))
    for away, block in enumerate(blocks):
        value = block[...].reshape(flat, LANES)
        at = pl.ds(pl.multiple_of((place[0] ^ away) * LANES, LANES), LANES)
        hi_ref[:flat, at], lo_ref[:flat, at] = split(value)
        hi_ref[flat:, at], lo_ref[flat:, at] = split(sign * swap(value))
    sums = dot3((hi_ref[...], lo_ref[...]), (t_hi[...], t_lo[...]))
    legs = []
    for k0 in range(RADIX):
        real = sums[k0 * rows : (k0 + 1) * rows]
        imag = sums[flat + k0 * rows : flat + (k0 + 1) * rows]
        if k0 > 0:
            real, imag = times(tw[k0 : k0 + 1], -tw[RADIX + k0 : RADIX + k0 + 1], real, imag)
        legs.append((real, imag))
    (r0, i0), (r1, i1), (r2, i2), (r3, i3) = legs
    even_r, even_i, gap_r, gap_i = r0 + r2, i0 + i2, r0 - r2, i0 - i2
    odd_r, odd_i, skew_r, skew_i = r1 + r3, i1 + i3, r1 - r3, i1 - i3
    results = [
        (even_r + odd_r, even_i + odd_i),
        (gap_r - skew_i, gap_i + skew_r),
        (even_r - odd_r, even_i - odd_i),
        (gap_r + skew_i, gap_i - skew_r),
    ]
    for a, (real, imag) in enumerate(results):
        out[0, 0, :, a * SPAN : (a + 1) * SPAN] = real
        out[0, 1, :, a * SPAN : (a + 1) * SPAN] = imag


def unsort_kernel(blocks, order, *refs):
    out = refs[-1]
    rows = out.shape[2]
    for component in range(2):
        real, imag = [], []
        for pair in range(RADIX // 2):
            at = component * RADIX + 2 * pair
            halves_of = paired(blocks[at], blocks[at + 1])
            real.append(halves_of[0])
            imag.append(halves_of[1])
        flat = jnp.concatenate([jnp.concatenate(real, axis=1), jnp.concatenate(imag, axis=1)], axis=0)
        far = moved(flat, order[...])
        out[component, 0] = far[:rows]
        out[component, 1] = far[rows:]


ALONE = pltpu.CompilerParams(vmem_limit_bytes=60 * 1024 * 1024)
SHARED = pltpu.CompilerParams(vmem_limit_bytes=24 * 1024 * 1024)


COST = pl.CostEstimate(flops=1 << 20, bytes_accessed=1 << 16, transcendentals=0)


def whole(kernel, shapes, *args, after=(), params=SHARED):
    shapes = [jax.ShapeDtypeStruct(shape, f32) for shape in shapes]
    in_vmem = pl.BlockSpec(memory_space=pltpu.VMEM)
    result = pl.pallas_call(
        kernel,
        out_shape=shapes,
        in_specs=[in_vmem] * len(args) + [pl.BlockSpec(memory_space=pl.ANY)] * len(after),
        out_specs=[in_vmem] * len(shapes),
        compiler_params=params,
        cost_estimate=COST,
    )(*args, *after)
    return result if len(shapes) > 1 else result[0]


def onward_kernel(blocks, far, near, *refs):
    refs[-2][...] = blocks[...] + far[...]
    refs[-1][...] = near[...]


def total_kernel(own, near, skip, half, *refs):
    out, first, second = refs[-3:]
    out[...] = (own[...] + near[...]) + skip[...]
    first[...] = half[:RADIX]
    second[...] = half[RADIX:]


def fixed(shape):
    return pl.BlockSpec(shape, lambda *_: (0,) * len(shape))


def start(place, currents, far_gradient, shards, tables):
    rows, columns = currents.shape[2:]
    tile = rows // 2
    t_hi, t_lo = tables["x"]
    sorted_shape = (2 * RADIX, far_gradient.shape[2], LANES)
    return pl.pallas_call(
        functools.partial(start_kernel, shards),
        grid_spec=pltpu.PrefetchScalarGridSpec(
            num_scalar_prefetch=1,
            grid=(2, rows // tile),
            in_specs=[
                pl.BlockSpec((1, 2, tile, columns), lambda c, i, _: (c, 0, i, 0)),
                fixed((2 * RADIX, SPAN)),
                fixed(t_hi.shape),
                fixed(t_lo.shape),
                fixed(far_gradient.shape),
                fixed(tables["order"].shape),
            ],
            out_specs=[fixed(sorted_shape)]
            + [pl.BlockSpec((RADIX, tile, LANES), lambda c, i, _: (c, i, 0))] * shards,
            scratch_shapes=[pltpu.VMEM((shards, RADIX, tile, LANES), f32)],
        ),
        out_shape=[jax.ShapeDtypeStruct(sorted_shape, f32)]
        + [jax.ShapeDtypeStruct((2 * RADIX, rows, LANES), f32)] * shards,
        compiler_params=ALONE,
        cost_estimate=COST,
    )(place, currents, tables["row_tw"], t_hi, t_lo, far_gradient, tables["order"])


def back_x(place, parts, component, grad, shape, tables):
    rows = shape[2]
    tile = rows // 2
    t_hi, t_lo = tables["x_back"]
    both = pl.BlockSpec((RADIX, tile, LANES), lambda i, _: (component, i, 0))
    one = pl.BlockSpec((RADIX, tile, LANES), lambda i, _: (0, i, 0))
    first = grad is None
    return pl.pallas_call(
        x_back_kernel,
        grid_spec=pltpu.PrefetchScalarGridSpec(
            num_scalar_prefetch=1,
            grid=(rows // tile,),
            in_specs=[pl.BlockSpec(memory_space=pl.ANY)]
            + [both if part.shape[0] > RADIX else one for part in parts]
            + [fixed((2 * RADIX, SPAN)), fixed(t_hi.shape), fixed(t_lo.shape)],
            out_specs=pl.BlockSpec((1, 2, tile, shape[3]), lambda i, _: (component, 0, i, 0)),
            scratch_shapes=[
                pltpu.VMEM((2 * RADIX * tile, 2 * BANDS), bf16),
                pltpu.VMEM((2 * RADIX * tile, 2 * BANDS), bf16),
            ],
        ),
        out_shape=jax.ShapeDtypeStruct(shape, f32),
        input_output_aliases={} if first else {1: 0},
        compiler_params=SHARED,
        cost_estimate=COST,
    )(place, tables["row_tw"] if first else grad, *parts, tables["row_tw"], t_hi, t_lo)


PAIRS = [(0, 1), (1, 0), (2, 3), (3, 2)]
SKIPS = [(0, 2), (2, 0), (1, 3), (3, 1)]


def send(value, pairs):
    return lax.ppermute(value, "narrow", pairs)


def fast_body(tables, currents, far_gradient):
    shards = lax.axis_size("narrow")
    wide = lax.axis_size("wide")
    rows = currents.shape[2]
    angle_rows = far_gradient.shape[2]
    scale = 1.0 / math.sqrt(rows * wide * NX)
    place = lax.axis_index("narrow").astype(jnp.int32).reshape(1)
    y_hi, y_lo = tables["y"]
    b_hi, b_lo = tables["y_back"]

    group = (RADIX, rows, LANES)
    sorted_, *blocks = start(place, currents, far_gradient, shards, tables)
    far = send(blocks[3], PAIRS)

    onward, close = whole(onward_kernel, [blocks[0].shape] * 2, blocks[2], far, blocks[1])
    skip = send(onward, SKIPS)
    near = send(close, PAIRS)

    rows_in = lax.all_to_all(sorted_, "wide", 0, 0).reshape(MY, LANES)
    rows_out = whole(
        functools.partial(y_back_kernel, scale),
        [(rows * wide, LANES)],
        rows_in,
        tables["col_tw"],
        b_hi,
        b_lo,
        after=[onward],
    )
    half = lax.all_to_all(rows_out.reshape(wide, rows, LANES), "wide", 0, 0)

    beside = send(half, PAIRS)
    columns, *mine = whole(
        total_kernel, [blocks[0].shape, group, group], blocks[0], near, skip, half
    )

    there = [send(m, SKIPS) for m in mine]

    rows_in = lax.all_to_all(columns, "wide", 0, 0).reshape(rows * wide, LANES)
    rows_out = whole(
        functools.partial(y_kernel, scale),
        [(MY, LANES)],
        rows_in,
        tables["col_tw"],
        y_hi,
        y_lo,
    )
    far = lax.all_to_all(rows_out.reshape(wide, angle_rows, LANES), "wide", 0, 0)

    across = [send(t, PAIRS) for t in there]
    far_field = whole(unsort_kernel, [far_gradient.shape], far, tables["order_back"])
    grad = None
    for c in range(2):
        grad = back_x(place, [half, beside, there[c], across[c]], c, grad, currents.shape, tables)
    return (far_field, grad)


def solution(mesh):
    spec = P(None, None, "wide", "narrow")
    shards, wide = mesh.shape["narrow"], mesh.shape["wide"]

    def run(currents, far_gradient):
        rows = currents.shape[2]
        fits = (
            shards == 4
            and currents.shape[3] == shards * PERIOD
            and rows == 2 * SPAN
            and far_gradient.shape[2] == MY == 2 * SPAN
            and BANDS // shards == HALF
            and wide == 2 * RADIX
        )
        body = functools.partial(fast_body, make_tables(shards)) if fits else general_body
        return jax.shard_map(
            body, mesh=mesh, in_specs=(spec, spec), out_specs=(spec, spec), check_vma=False
        )(currents, far_gradient)

    return run
```

```python
import functools
import math

import jax
import jax.numpy as jnp
import numpy as np
from jax import lax
from jax.experimental import pallas as pl
from jax.experimental.pallas import tpu as pltpu
from jax.sharding import PartitionSpec as P

NX = 8192
MX = 1024
MY = 1024
STRIDE = 4

PERIOD = NX // STRIDE
RADIX = 4
SPAN = PERIOD // RADIX
BANDS = MX // RADIX
LANES = 128
HALF = LANES // 2

f32 = jnp.float32
bf16 = jnp.bfloat16
precise = lax.Precision.HIGHEST


def phase_table(pos_start, pos_count, pos_total, ang_count, modulus):
    position = pos_start + jnp.arange(pos_count, dtype=jnp.int32) - pos_total // 2
    angles = jnp.arange(ang_count, dtype=jnp.int32) - ang_count // 2
    cycles = jnp.mod(position[:, None] * angles[None, :] * STRIDE, modulus)
    radians = 2.0 * math.pi / modulus * cycles.astype(jnp.float32)
    return (jnp.cos(radians), jnp.sin(radians))


def contract(left, right, left_dim, right_dim):
    return lax.dot_general(
        left,
        right,
        (((left_dim,), (right_dim,)), ((), ())),
        precision=precise,
        preferred_element_type=jnp.float32,
    )


def general_body(currents, far_gradient):
    row_count = currents.shape[2]
    column_count = currents.shape[3]
    angle_rows = far_gradient.shape[2]
    angle_cols = far_gradient.shape[3]
    total_rows = row_count * lax.axis_size("wide")
    scale = 1.0 / math.sqrt(total_rows * NX)
    row_start = lax.axis_index("wide") * row_count
    column_start = lax.axis_index("narrow") * column_count
    cos_x, sin_x = phase_table(column_start, column_count, NX, MX, NX)
    cos_y, sin_y = phase_table(row_start, row_count, total_rows, MY, NX)
    real_cur = currents[:, 0].reshape(2 * row_count, column_count)
    imag_cur = currents[:, 1].reshape(2 * row_count, column_count)
    real_term = contract(cos_x, real_cur, 0, 1) + contract(sin_x, imag_cur, 0, 1)
    imag_term = contract(cos_x, imag_cur, 0, 1) - contract(sin_x, real_cur, 0, 1)
    column_sums = lax.psum_scatter(
        jnp.stack([real_term, imag_term], axis=1), "narrow", scatter_dimension=0, tiled=True
    )
    sum_real = column_sums[:, 0].reshape(angle_cols * 2, row_count)
    sum_imag = column_sums[:, 1].reshape(angle_cols * 2, row_count)
    real_term = contract(cos_y, sum_real, 0, 1) + contract(sin_y, sum_imag, 0, 1)
    imag_term = contract(cos_y, sum_imag, 0, 1) - contract(sin_y, sum_real, 0, 1)
    far_sums = lax.psum_scatter(
        scale * jnp.stack([real_term, imag_term], axis=1), "wide", scatter_dimension=0, tiled=True
    )
    far_field = far_sums.reshape(angle_rows, 2, angle_cols, 2).transpose(3, 1, 0, 2)
    grad_real = far_gradient[:, 0].transpose(1, 2, 0).reshape(angle_rows, angle_cols * 2)
    grad_imag = far_gradient[:, 1].transpose(1, 2, 0).reshape(angle_rows, angle_cols * 2)
    piece_real = lax.all_gather(grad_real, "wide", axis=0, tiled=True)
    piece_imag = lax.all_gather(grad_imag, "wide", axis=0, tiled=True)
    half_real = contract(piece_real, cos_y, 0, 1) - contract(piece_imag, sin_y, 0, 1)
    half_imag = contract(piece_imag, cos_y, 0, 1) + contract(piece_real, sin_y, 0, 1)
    half_real = half_real.reshape(angle_cols, 2, row_count)
    half_imag = half_imag.reshape(angle_cols, 2, row_count)
    piece_real = lax.all_gather(half_real, "narrow", axis=0, tiled=True)
    piece_imag = lax.all_gather(half_imag, "narrow", axis=0, tiled=True)
    width = piece_real.shape[0]
    flat_real = piece_real.reshape(width, 2 * row_count)
    flat_imag = piece_imag.reshape(width, 2 * row_count)
    back_real = contract(flat_real, cos_x, 0, 1) - contract(flat_imag, sin_x, 0, 1)
    back_imag = contract(flat_imag, cos_x, 0, 1) + contract(flat_real, sin_x, 0, 1)
    back_real = back_real.reshape(2, row_count, column_count)
    back_imag = back_imag.reshape(2, row_count, column_count)
    aperture_grad = scale * jnp.stack([back_real, back_imag], axis=1)
    return (far_field, aperture_grad)


def halves(table):
    hi = table.astype(np.float32).astype(bf16)
    return hi, (table - hi.astype(np.float64)).astype(np.float32).astype(bf16)


def angle(count_left, left_start, count_right, right_start, period):
    left = np.arange(count_left, dtype=np.int64) + left_start
    right = np.arange(count_right, dtype=np.int64) + right_start
    return 2.0 * np.pi / period * ((left[:, None] * right[None, :]) % period)


def make_tables(shards):
    theta = angle(SPAN, 0, BANDS, -(BANDS // 2), SPAN)
    cos, sin = np.cos(theta), np.sin(theta)
    each = BANDS // shards
    x_table = np.stack([cos.reshape(SPAN, shards, each), -sin.reshape(SPAN, shards, each)], axis=2)
    x_table = x_table.reshape(SPAN, 2 * BANDS)
    y_table = np.concatenate([cos.T, sin.T], axis=0)
    y_back = np.concatenate([cos, sin], axis=0)
    twiddle = angle(RADIX, 0, SPAN, 0, PERIOD)
    cols = RADIX * each
    order = np.zeros((each, RADIX, RADIX, each))
    for k0 in range(RADIX):
        order[np.arange(each), k0, k0, np.arange(each)] = 1.0
    order = order.reshape(cols, cols).astype(bf16)
    return {
        "x": halves(x_table),
        "x_back": halves(np.ascontiguousarray(x_table.T)),
        "y": halves(y_table),
        "y_back": halves(y_back),
        "row_tw": np.concatenate([np.cos(twiddle), np.sin(twiddle)], axis=0).astype(np.float32),
        "col_tw": np.ascontiguousarray(
            np.concatenate([np.cos(twiddle), np.sin(twiddle)], axis=0).T
        ).astype(np.float32),
        "order": order,
        "order_back": np.ascontiguousarray(order.T),
    }


def split(value):
    hi = value.astype(bf16)
    return hi, (value - hi.astype(f32)).astype(bf16)


def dot(left, right):
    return jnp.dot(left, right, preferred_element_type=f32)


def dot3(left, right):
    return dot(left[0], right[0]) + (dot(left[1], right[0]) + dot(left[0], right[1]))


def times(tw_cos, tw_sin, real, imag):
    return real * tw_cos + imag * tw_sin, imag * tw_cos - real * tw_sin


def sign_of(shape):
    lane = lax.broadcasted_iota(jnp.int32, shape, len(shape) - 1)
    return jnp.where(lane < HALF, 1.0, -1.0).astype(f32)


def swap(value):
    return pltpu.roll(value, HALF, axis=1)


def moved(value, order):
    hi = value.astype(bf16)
    rest = value - hi.astype(f32)
    mid = rest.astype(bf16)
    lo = (rest - mid.astype(f32)).astype(bf16)
    return dot(hi, order) + (dot(mid, order) + dot(lo, order))


def paired(first, second):
    left = lax.broadcasted_iota(jnp.int32, first.shape, 1) < HALF
    return jnp.where(left, first, swap(second)), jnp.where(left, swap(first), second)


def sort(grad, order, out):
    rows = grad.shape[2]
    for component in range(2):
        flat = jnp.concatenate([grad[component, 0], grad[component, 1]], axis=0)
        places = moved(flat, order[...])
        for pair in range(RADIX // 2):
            lanes = places[:, pair * LANES : (pair + 1) * LANES]
            at = component * RADIX + 2 * pair
            out[at], out[at + 1] = paired(lanes[:rows], lanes[rows:])


def x_kernel(shards, place, cur, tw, t_hi, t_lo, *refs):
    outs, held = refs[-shards - 1 : -1], refs[-1]
    rows = cur.shape[2]

    if len(refs) > shards + 1:

        @pl.when(pl.program_id(0) == 0)
        def _():
            sort(*refs[1:4])

    re = [cur[0, 0, :, a * SPAN : (a + 1) * SPAN] for a in range(RADIX)]
    im = [cur[0, 1, :, a * SPAN : (a + 1) * SPAN] for a in range(RADIX)]
    sum_re, dif_re = re[0] + re[2], re[0] - re[2]
    sum_im, dif_im = im[0] + im[2], im[0] - im[2]
    odd_re, gap_re = re[1] + re[3], re[1] - re[3]
    odd_im, gap_im = im[1] + im[3], im[1] - im[3]
    legs = [
        (sum_re + odd_re, sum_im + odd_im),
        (dif_re + gap_im, dif_im - gap_re),
        (sum_re - odd_re, sum_im - odd_im),
        (dif_re - gap_im, dif_im + gap_re),
    ]
    flat = []
    for k0, (real, imag) in enumerate(legs):
        if k0 > 0:
            real, imag = times(tw[k0 : k0 + 1], tw[RADIX + k0 : RADIX + k0 + 1], real, imag)
        flat += [real, imag]
    sums = dot3(split(jnp.concatenate(flat, axis=0)), (t_hi[...], t_lo[...]))
    sign = sign_of((rows, LANES))
    for shard in range(shards):
        lanes = sums[:, shard * LANES : (shard + 1) * LANES]
        for k0 in range(RADIX):
            of_real = lanes[2 * k0 * rows : (2 * k0 + 1) * rows]
            of_imag = lanes[(2 * k0 + 1) * rows : (2 * k0 + 2) * rows]
            held[shard, k0] = of_real - sign * swap(of_imag)
    for away, out in enumerate(outs):
        out[...] = held[place[0] ^ away]


def y_kernel(scale, col, tw, t_hi, t_lo, *refs):
    out = refs[-1]
    early, late = col[:SPAN], col[SPAN:]
    sign = sign_of(early.shape)
    turned = sign * swap(early)
    flat = []
    for k0, leg in enumerate([late + early, late - turned, late - early, late + turned]):
        if k0 > 0:
            leg = leg * tw[:, k0 : k0 + 1] + (sign * tw[:, RADIX + k0 : RADIX + k0 + 1]) * swap(leg)
        flat.append(leg)
    hi, lo = split(jnp.concatenate(flat, axis=1))
    both = dot3((t_hi[...], t_lo[...]), (hi, lo))
    half_sign = scale * sign_of((BANDS, LANES))
    for k0 in range(RADIX):
        cos_part = both[:BANDS, k0 * LANES : (k0 + 1) * LANES]
        sin_part = both[BANDS:, k0 * LANES : (k0 + 1) * LANES]
        out[pl.ds(k0, BANDS, stride=RADIX), :] = scale * cos_part + half_sign * swap(sin_part)


def y_back_kernel(scale, grad, tw, t_hi, t_lo, *refs):
    out = refs[-1]
    flat = [grad[pl.ds(k0, BANDS, stride=RADIX), :] for k0 in range(RADIX)]
    hi, lo = split(jnp.concatenate(flat, axis=1))
    both = dot3((t_hi[...], t_lo[...]), (hi, lo))
    sign = sign_of((SPAN, LANES))
    legs = []
    for k0 in range(RADIX):
        cos_part = both[:SPAN, k0 * LANES : (k0 + 1) * LANES]
        sin_part = both[SPAN:, k0 * LANES : (k0 + 1) * LANES]
        leg = cos_part - sign * swap(sin_part)
        if k0 > 0:
            leg = leg * tw[:, k0 : k0 + 1] - (sign * tw[:, RADIX + k0 : RADIX + k0 + 1]) * swap(leg)
        legs.append(leg)
    even, odd = legs[0] + legs[2], legs[1] + legs[3]
    out[SPAN:, :] = scale * (even + odd)
    out[:SPAN, :] = scale * ((legs[0] - legs[2]) + sign * swap(legs[1] - legs[3]))


def x_back_kernel(place, _, *refs):
    blocks, (tw, t_hi, t_lo, out, done, hi_ref, lo_ref) = refs[:-7], refs[-7:]
    done[...] = jnp.zeros(done.shape, f32)
    rows = out.shape[2]
    flat = RADIX * rows
    sign = sign_of((flat, LANES))
    for away, block in enumerate(blocks):
        value = block[...].reshape(flat, LANES)
        at = pl.ds(pl.multiple_of((place[0] ^ away) * LANES, LANES), LANES)
        hi_ref[:flat, at], lo_ref[:flat, at] = split(value)
        hi_ref[flat:, at], lo_ref[flat:, at] = split(sign * swap(value))
    sums = dot3((hi_ref[...], lo_ref[...]), (t_hi[...], t_lo[...]))
    legs = []
    for k0 in range(RADIX):
        real = sums[k0 * rows : (k0 + 1) * rows]
        imag = sums[flat + k0 * rows : flat + (k0 + 1) * rows]
        if k0 > 0:
            real, imag = times(tw[k0 : k0 + 1], -tw[RADIX + k0 : RADIX + k0 + 1], real, imag)
        legs.append((real, imag))
    (r0, i0), (r1, i1), (r2, i2), (r3, i3) = legs
    even_r, even_i, gap_r, gap_i = r0 + r2, i0 + i2, r0 - r2, i0 - i2
    odd_r, odd_i, skew_r, skew_i = r1 + r3, i1 + i3, r1 - r3, i1 - i3
    results = [
        (even_r + odd_r, even_i + odd_i),
        (gap_r - skew_i, gap_i + skew_r),
        (even_r - odd_r, even_i - odd_i),
        (gap_r + skew_i, gap_i - skew_r),
    ]
    for a, (real, imag) in enumerate(results):
        out[0, 0, :, a * SPAN : (a + 1) * SPAN] = real
        out[0, 1, :, a * SPAN : (a + 1) * SPAN] = imag


def unsort_kernel(blocks, order, *refs):
    out = refs[-1]
    rows = out.shape[2]
    for component in range(2):
        real, imag = [], []
        for pair in range(RADIX // 2):
            at = component * RADIX + 2 * pair
            halves_of = paired(blocks[at], blocks[at + 1])
            real.append(halves_of[0])
            imag.append(halves_of[1])
        flat = jnp.concatenate([jnp.concatenate(real, axis=1), jnp.concatenate(imag, axis=1)], axis=0)
        far = moved(flat, order[...])
        out[component, 0] = far[:rows]
        out[component, 1] = far[rows:]


ALONE = pltpu.CompilerParams(vmem_limit_bytes=60 * 1024 * 1024)
SHARED = pltpu.CompilerParams(vmem_limit_bytes=24 * 1024 * 1024)


COST = pl.CostEstimate(flops=1 << 20, bytes_accessed=1 << 16, transcendentals=0)


LONG = pl.CostEstimate(flops=1 << 37, bytes_accessed=1 << 29, transcendentals=0)


def whole(kernel, shapes, *args, after=(), params=SHARED, cost=COST):
    shapes = [jax.ShapeDtypeStruct(shape, f32) for shape in shapes]
    in_vmem = pl.BlockSpec(memory_space=pltpu.VMEM)
    result = pl.pallas_call(
        kernel,
        out_shape=shapes,
        in_specs=[in_vmem] * len(args) + [pl.BlockSpec(memory_space=pl.ANY)] * len(after),
        out_specs=[in_vmem] * len(shapes),
        compiler_params=params,
        cost_estimate=cost,
    )(*args, *after)
    return result if len(shapes) > 1 else result[0]


def zero_kernel(*refs):
    refs[-1][...] = jnp.zeros(refs[-1].shape, f32)


def zeros_after(*arrays):
    return whole(zero_kernel, [(8, LANES)], after=arrays, cost=LONG)


def halves_kernel(both, *refs):
    first, second = refs[-2:]
    first[...] = both[:RADIX]
    second[...] = both[RADIX:]


def fixed(shape):
    return pl.BlockSpec(shape, lambda *_: (0,) * len(shape))


def project_x(place, currents, component, shards, tables, far_gradient=None, after=None):
    rows, columns = currents.shape[2:]
    tile = rows // 2
    t_hi, t_lo = tables["x"]
    args = [place, currents, tables["row_tw"], t_hi, t_lo]
    in_specs = [
        pl.BlockSpec((1, 2, tile, columns), lambda i, _: (component, 0, i, 0)),
        fixed((2 * RADIX, SPAN)),
        fixed(t_hi.shape),
        fixed(t_lo.shape),
    ]
    out_specs = [pl.BlockSpec((RADIX, tile, LANES), lambda i, _: (0, i, 0))] * shards
    shapes = [(RADIX, rows, LANES)] * shards
    if far_gradient is not None:
        args += [after, far_gradient, tables["order"]]
        in_specs += [pl.BlockSpec(memory_space=pl.ANY)]
        in_specs += [fixed(far_gradient.shape), fixed(tables["order"].shape)]
        shapes.insert(0, (2 * RADIX, far_gradient.shape[2], LANES))
        out_specs.insert(0, fixed(shapes[0]))
    return pl.pallas_call(
        functools.partial(x_kernel, shards),
        grid_spec=pltpu.PrefetchScalarGridSpec(
            num_scalar_prefetch=1,
            grid=(rows // tile,),
            in_specs=in_specs,
            out_specs=out_specs,
            scratch_shapes=[pltpu.VMEM((shards, RADIX, tile, LANES), f32)],
        ),
        out_shape=[jax.ShapeDtypeStruct(shape, f32) for shape in shapes],
        compiler_params=ALONE,
        cost_estimate=COST,
    )(*args)


def back_x(place, parts, component, grad, shape, tables):
    rows = shape[2]
    tile = rows // 2
    t_hi, t_lo = tables["x_back"]
    both = pl.BlockSpec((RADIX, tile, LANES), lambda i, _: (component, i, 0))
    one = pl.BlockSpec((RADIX, tile, LANES), lambda i, _: (0, i, 0))
    first = grad is None
    return pl.pallas_call(
        x_back_kernel,
        grid_spec=pltpu.PrefetchScalarGridSpec(
            num_scalar_prefetch=1,
            grid=(rows // tile,),
            in_specs=[pl.BlockSpec(memory_space=pl.ANY)]
            + [both if part.shape[0] > RADIX else one for part in parts]
            + [fixed((2 * RADIX, SPAN)), fixed(t_hi.shape), fixed(t_lo.shape)],
            out_specs=[
                pl.BlockSpec((1, 2, tile, shape[3]), lambda i, _: (component, 0, i, 0)),
                fixed((8, LANES)),
            ],
            scratch_shapes=[
                pltpu.VMEM((2 * RADIX * tile, 2 * BANDS), bf16),
                pltpu.VMEM((2 * RADIX * tile, 2 * BANDS), bf16),
            ],
        ),
        out_shape=[jax.ShapeDtypeStruct(shape, f32), jax.ShapeDtypeStruct((8, LANES), f32)],
        input_output_aliases={} if first else {1: 0},
        compiler_params=SHARED,
        cost_estimate=LONG if first else COST,
    )(place, tables["row_tw"] if first else grad, *parts, tables["row_tw"], t_hi, t_lo)


PAIRS = [(0, 1), (1, 0), (2, 3), (3, 2)]
SKIPS = [(0, 2), (2, 0), (1, 3), (3, 1)]


def send(value, pairs):
    return lax.ppermute(value, "narrow", pairs)


def fast_body(tables, currents, far_gradient):
    shards = lax.axis_size("narrow")
    wide = lax.axis_size("wide")
    rows = currents.shape[2]
    angle_rows = far_gradient.shape[2]
    scale = 1.0 / math.sqrt(rows * wide * NX)
    place = lax.axis_index("narrow").astype(jnp.int32).reshape(1)
    y_hi, y_lo = tables["y"]
    b_hi, b_lo = tables["y_back"]

    group = (RADIX, rows, LANES)
    blocks = [project_x(place, currents, 0, shards, tables)]
    far = [send(blocks[0][3], PAIRS)]
    sorted_, *rest = project_x(
        place, currents, 1, shards, tables, far_gradient, blocks[0][0]
    )
    blocks.append(rest)
    far.append(send(blocks[1][3], PAIRS))
    later = zeros_after(far[0])[0, 0]
    onward = jnp.concatenate([blocks[0][2] + far[0], blocks[1][2] + far[1] + later], axis=0)
    skip = send(onward, SKIPS)
    near = send(jnp.concatenate([blocks[c][1] + later for c in range(2)], axis=0), PAIRS)

    rows_in = lax.all_to_all(sorted_, "wide", 0, 0).reshape(MY, LANES)
    rows_out = whole(
        functools.partial(y_back_kernel, scale),
        [(rows * wide, LANES)],
        rows_in,
        tables["col_tw"],
        b_hi,
        b_lo,
        after=[onward],
    )
    half = lax.all_to_all(rows_out.reshape(wide, rows, LANES), "wide", 0, 0)
    beside = send(half, PAIRS)

    columns = jnp.concatenate([blocks[c][0] for c in range(2)], axis=0) + near + skip
    columns = columns + zeros_after(near)[0, 0]

    mine = whole(halves_kernel, [group, group], half, after=[columns])
    there = [send(m, SKIPS) for m in mine]

    rows_in = lax.all_to_all(columns, "wide", 0, 0).reshape(rows * wide, LANES)
    rows_out = whole(
        functools.partial(y_kernel, scale),
        [(MY, LANES)],
        rows_in,
        tables["col_tw"],
        y_hi,
        y_lo,
        after=[zeros_after(there[0], beside)],
    )
    far = lax.all_to_all(rows_out.reshape(wide, angle_rows, LANES), "wide", 0, 0)

    across = [send(t, PAIRS) for t in there]
    grad, _ = back_x(place, [mine[0], beside, there[0], across[0]], 0, None, currents.shape, tables)
    far_field = whole(unsort_kernel, [far_gradient.shape], far, tables["order_back"])
    grad, _ = back_x(place, [mine[1], beside, there[1], across[1]], 1, grad, currents.shape, tables)
    return (far_field, grad)


def solution(mesh):
    spec = P(None, None, "wide", "narrow")
    shards, wide = mesh.shape["narrow"], mesh.shape["wide"]

    def run(currents, far_gradient):
        rows = currents.shape[2]
        fits = (
            shards == 4
            and currents.shape[3] == shards * PERIOD
            and rows == 2 * SPAN
            and far_gradient.shape[2] == MY == 2 * SPAN
            and BANDS // shards == HALF
            and wide == 2 * RADIX
        )
        body = functools.partial(fast_body, make_tables(shards)) if fits else general_body
        return jax.shard_map(
            body, mesh=mesh, in_specs=(spec, spec), out_specs=(spec, spec), check_vma=False
        )(currents, far_gradient)

    return run
```

```python
import functools
import math

import jax
import jax.numpy as jnp
import numpy as np
from jax import lax
from jax.experimental import pallas as pl
from jax.experimental.pallas import tpu as pltpu
from jax.sharding import PartitionSpec as P

NX = 8192
MX = 1024
MY = 1024
STRIDE = 4

PERIOD = NX // STRIDE
RADIX = 4
SPAN = PERIOD // RADIX
BANDS = MX // RADIX
LANES = 128
HALF = LANES // 2

f32 = jnp.float32
bf16 = jnp.bfloat16
precise = lax.Precision.HIGHEST


def phase_table(pos_start, pos_count, pos_total, ang_count, modulus):
    position = pos_start + jnp.arange(pos_count, dtype=jnp.int32) - pos_total // 2
    angles = jnp.arange(ang_count, dtype=jnp.int32) - ang_count // 2
    cycles = jnp.mod(position[:, None] * angles[None, :] * STRIDE, modulus)
    radians = 2.0 * math.pi / modulus * cycles.astype(jnp.float32)
    return (jnp.cos(radians), jnp.sin(radians))


def contract(left, right, left_dim, right_dim):
    return lax.dot_general(
        left,
        right,
        (((left_dim,), (right_dim,)), ((), ())),
        precision=precise,
        preferred_element_type=jnp.float32,
    )


def general_body(currents, far_gradient):
    row_count = currents.shape[2]
    column_count = currents.shape[3]
    angle_rows = far_gradient.shape[2]
    angle_cols = far_gradient.shape[3]
    total_rows = row_count * lax.axis_size("wide")
    scale = 1.0 / math.sqrt(total_rows * NX)
    row_start = lax.axis_index("wide") * row_count
    column_start = lax.axis_index("narrow") * column_count
    cos_x, sin_x = phase_table(column_start, column_count, NX, MX, NX)
    cos_y, sin_y = phase_table(row_start, row_count, total_rows, MY, NX)
    real_cur = currents[:, 0].reshape(2 * row_count, column_count)
    imag_cur = currents[:, 1].reshape(2 * row_count, column_count)
    real_term = contract(cos_x, real_cur, 0, 1) + contract(sin_x, imag_cur, 0, 1)
    imag_term = contract(cos_x, imag_cur, 0, 1) - contract(sin_x, real_cur, 0, 1)
    column_sums = lax.psum_scatter(
        jnp.stack([real_term, imag_term], axis=1), "narrow", scatter_dimension=0, tiled=True
    )
    sum_real = column_sums[:, 0].reshape(angle_cols * 2, row_count)
    sum_imag = column_sums[:, 1].reshape(angle_cols * 2, row_count)
    real_term = contract(cos_y, sum_real, 0, 1) + contract(sin_y, sum_imag, 0, 1)
    imag_term = contract(cos_y, sum_imag, 0, 1) - contract(sin_y, sum_real, 0, 1)
    far_sums = lax.psum_scatter(
        scale * jnp.stack([real_term, imag_term], axis=1), "wide", scatter_dimension=0, tiled=True
    )
    far_field = far_sums.reshape(angle_rows, 2, angle_cols, 2).transpose(3, 1, 0, 2)
    grad_real = far_gradient[:, 0].transpose(1, 2, 0).reshape(angle_rows, angle_cols * 2)
    grad_imag = far_gradient[:, 1].transpose(1, 2, 0).reshape(angle_rows, angle_cols * 2)
    piece_real = lax.all_gather(grad_real, "wide", axis=0, tiled=True)
    piece_imag = lax.all_gather(grad_imag, "wide", axis=0, tiled=True)
    half_real = contract(piece_real, cos_y, 0, 1) - contract(piece_imag, sin_y, 0, 1)
    half_imag = contract(piece_imag, cos_y, 0, 1) + contract(piece_real, sin_y, 0, 1)
    half_real = half_real.reshape(angle_cols, 2, row_count)
    half_imag = half_imag.reshape(angle_cols, 2, row_count)
    piece_real = lax.all_gather(half_real, "narrow", axis=0, tiled=True)
    piece_imag = lax.all_gather(half_imag, "narrow", axis=0, tiled=True)
    width = piece_real.shape[0]
    flat_real = piece_real.reshape(width, 2 * row_count)
    flat_imag = piece_imag.reshape(width, 2 * row_count)
    back_real = contract(flat_real, cos_x, 0, 1) - contract(flat_imag, sin_x, 0, 1)
    back_imag = contract(flat_imag, cos_x, 0, 1) + contract(flat_real, sin_x, 0, 1)
    back_real = back_real.reshape(2, row_count, column_count)
    back_imag = back_imag.reshape(2, row_count, column_count)
    aperture_grad = scale * jnp.stack([back_real, back_imag], axis=1)
    return (far_field, aperture_grad)


def halves(table):
    hi = table.astype(np.float32).astype(bf16)
    return hi, (table - hi.astype(np.float64)).astype(np.float32).astype(bf16)


def angle(count_left, left_start, count_right, right_start, period):
    left = np.arange(count_left, dtype=np.int64) + left_start
    right = np.arange(count_right, dtype=np.int64) + right_start
    return 2.0 * np.pi / period * ((left[:, None] * right[None, :]) % period)


def make_tables(shards):
    theta = angle(SPAN, 0, BANDS, -(BANDS // 2), SPAN)
    cos, sin = np.cos(theta), np.sin(theta)
    each = BANDS // shards
    x_table = np.stack([cos.reshape(SPAN, shards, each), -sin.reshape(SPAN, shards, each)], axis=2)
    x_table = x_table.reshape(SPAN, 2 * BANDS)
    y_table = np.concatenate([cos.T, sin.T], axis=0)
    y_back = np.concatenate([cos, sin], axis=0)
    twiddle = angle(RADIX, 0, SPAN, 0, PERIOD)
    cols = RADIX * each
    order = np.zeros((each, RADIX, RADIX, each))
    for k0 in range(RADIX):
        order[np.arange(each), k0, k0, np.arange(each)] = 1.0
    order = order.reshape(cols, cols).astype(bf16)
    return {
        "x": halves(x_table),
        "x_back": halves(np.ascontiguousarray(x_table.T)),
        "y": halves(y_table),
        "y_back": halves(y_back),
        "row_tw": np.concatenate([np.cos(twiddle), np.sin(twiddle)], axis=0).astype(np.float32),
        "col_tw": np.ascontiguousarray(
            np.concatenate([np.cos(twiddle), np.sin(twiddle)], axis=0).T
        ).astype(np.float32),
        "order": order,
        "order_back": np.ascontiguousarray(order.T),
    }


def split(value):
    hi = value.astype(bf16)
    return hi, (value - hi.astype(f32)).astype(bf16)


def dot(left, right):
    return jnp.dot(left, right, preferred_element_type=f32)


def dot3(left, right):
    return dot(left[0], right[0]) + (dot(left[1], right[0]) + dot(left[0], right[1]))


def times(tw_cos, tw_sin, real, imag):
    return real * tw_cos + imag * tw_sin, imag * tw_cos - real * tw_sin


def sign_of(shape):
    lane = lax.broadcasted_iota(jnp.int32, shape, len(shape) - 1)
    return jnp.where(lane < HALF, 1.0, -1.0).astype(f32)


def swap(value):
    return pltpu.roll(value, HALF, axis=1)


def moved(value, order):
    hi = value.astype(bf16)
    rest = value - hi.astype(f32)
    mid = rest.astype(bf16)
    lo = (rest - mid.astype(f32)).astype(bf16)
    return dot(hi, order) + (dot(mid, order) + dot(lo, order))


def paired(first, second):
    left = lax.broadcasted_iota(jnp.int32, first.shape, 1) < HALF
    return jnp.where(left, first, swap(second)), jnp.where(left, swap(first), second)


def sort(grad, order, out):
    rows = grad.shape[2]
    for component in range(2):
        flat = jnp.concatenate([grad[component, 0], grad[component, 1]], axis=0)
        places = moved(flat, order[...])
        for pair in range(RADIX // 2):
            lanes = places[:, pair * LANES : (pair + 1) * LANES]
            at = component * RADIX + 2 * pair
            out[at], out[at + 1] = paired(lanes[:rows], lanes[rows:])


def x_kernel(shards, place, cur, tw, t_hi, t_lo, *refs):
    outs, held = refs[-shards - 1 : -1], refs[-1]
    rows = cur.shape[2]

    if len(refs) > shards + 1:

        @pl.when(pl.program_id(0) == 0)
        def _():
            sort(*refs[1:4])

    re = [cur[0, 0, :, a * SPAN : (a + 1) * SPAN] for a in range(RADIX)]
    im = [cur[0, 1, :, a * SPAN : (a + 1) * SPAN] for a in range(RADIX)]
    sum_re, dif_re = re[0] + re[2], re[0] - re[2]
    sum_im, dif_im = im[0] + im[2], im[0] - im[2]
    odd_re, gap_re = re[1] + re[3], re[1] - re[3]
    odd_im, gap_im = im[1] + im[3], im[1] - im[3]
    legs = [
        (sum_re + odd_re, sum_im + odd_im),
        (dif_re + gap_im, dif_im - gap_re),
        (sum_re - odd_re, sum_im - odd_im),
        (dif_re - gap_im, dif_im + gap_re),
    ]
    flat = []
    for k0, (real, imag) in enumerate(legs):
        if k0 > 0:
            real, imag = times(tw[k0 : k0 + 1], tw[RADIX + k0 : RADIX + k0 + 1], real, imag)
        flat += [real, imag]
    sums = dot3(split(jnp.concatenate(flat, axis=0)), (t_hi[...], t_lo[...]))
    sign = sign_of((rows, LANES))
    for shard in range(shards):
        lanes = sums[:, shard * LANES : (shard + 1) * LANES]
        for k0 in range(RADIX):
            of_real = lanes[2 * k0 * rows : (2 * k0 + 1) * rows]
            of_imag = lanes[(2 * k0 + 1) * rows : (2 * k0 + 2) * rows]
            held[shard, k0] = of_real - sign * swap(of_imag)
    for away, out in enumerate(outs):
        out[...] = held[place[0] ^ away]


def y_kernel(scale, col, tw, t_hi, t_lo, *refs):
    out = refs[-1]
    early, late = col[:SPAN], col[SPAN:]
    sign = sign_of(early.shape)
    turned = sign * swap(early)
    flat = []
    for k0, leg in enumerate([late + early, late - turned, late - early, late + turned]):
        if k0 > 0:
            leg = leg * tw[:, k0 : k0 + 1] + (sign * tw[:, RADIX + k0 : RADIX + k0 + 1]) * swap(leg)
        flat.append(leg)
    hi, lo = split(jnp.concatenate(flat, axis=1))
    both = dot3((t_hi[...], t_lo[...]), (hi, lo))
    half_sign = scale * sign_of((BANDS, LANES))
    for k0 in range(RADIX):
        cos_part = both[:BANDS, k0 * LANES : (k0 + 1) * LANES]
        sin_part = both[BANDS:, k0 * LANES : (k0 + 1) * LANES]
        out[pl.ds(k0, BANDS, stride=RADIX), :] = scale * cos_part + half_sign * swap(sin_part)


def y_back_kernel(scale, grad, tw, t_hi, t_lo, *refs):
    out = refs[-1]
    flat = [grad[pl.ds(k0, BANDS, stride=RADIX), :] for k0 in range(RADIX)]
    hi, lo = split(jnp.concatenate(flat, axis=1))
    both = dot3((t_hi[...], t_lo[...]), (hi, lo))
    sign = sign_of((SPAN, LANES))
    legs = []
    for k0 in range(RADIX):
        cos_part = both[:SPAN, k0 * LANES : (k0 + 1) * LANES]
        sin_part = both[SPAN:, k0 * LANES : (k0 + 1) * LANES]
        leg = cos_part - sign * swap(sin_part)
        if k0 > 0:
            leg = leg * tw[:, k0 : k0 + 1] - (sign * tw[:, RADIX + k0 : RADIX + k0 + 1]) * swap(leg)
        legs.append(leg)
    even, odd = legs[0] + legs[2], legs[1] + legs[3]
    out[SPAN:, :] = scale * (even + odd)
    out[:SPAN, :] = scale * ((legs[0] - legs[2]) + sign * swap(legs[1] - legs[3]))


def x_back_kernel(place, _, *refs):
    blocks, (tw, t_hi, t_lo, out, done, hi_ref, lo_ref) = refs[:-7], refs[-7:]
    done[...] = jnp.zeros(done.shape, f32)
    rows = out.shape[2]
    flat = RADIX * rows
    sign = sign_of((flat, LANES))
    for away, block in enumerate(blocks):
        value = block[...].reshape(flat, LANES)
        at = pl.ds(pl.multiple_of((place[0] ^ away) * LANES, LANES), LANES)
        hi_ref[:flat, at], lo_ref[:flat, at] = split(value)
        hi_ref[flat:, at], lo_ref[flat:, at] = split(sign * swap(value))
    sums = dot3((hi_ref[...], lo_ref[...]), (t_hi[...], t_lo[...]))
    legs = []
    for k0 in range(RADIX):
        real = sums[k0 * rows : (k0 + 1) * rows]
        imag = sums[flat + k0 * rows : flat + (k0 + 1) * rows]
        if k0 > 0:
            real, imag = times(tw[k0 : k0 + 1], -tw[RADIX + k0 : RADIX + k0 + 1], real, imag)
        legs.append((real, imag))
    (r0, i0), (r1, i1), (r2, i2), (r3, i3) = legs
    even_r, even_i, gap_r, gap_i = r0 + r2, i0 + i2, r0 - r2, i0 - i2
    odd_r, odd_i, skew_r, skew_i = r1 + r3, i1 + i3, r1 - r3, i1 - i3
    results = [
        (even_r + odd_r, even_i + odd_i),
        (gap_r - skew_i, gap_i + skew_r),
        (even_r - odd_r, even_i - odd_i),
        (gap_r + skew_i, gap_i - skew_r),
    ]
    for a, (real, imag) in enumerate(results):
        out[0, 0, :, a * SPAN : (a + 1) * SPAN] = real
        out[0, 1, :, a * SPAN : (a + 1) * SPAN] = imag


def unsort_kernel(blocks, order, *refs):
    out = refs[-1]
    rows = out.shape[2]
    for component in range(2):
        real, imag = [], []
        for pair in range(RADIX // 2):
            at = component * RADIX + 2 * pair
            halves_of = paired(blocks[at], blocks[at + 1])
            real.append(halves_of[0])
            imag.append(halves_of[1])
        flat = jnp.concatenate([jnp.concatenate(real, axis=1), jnp.concatenate(imag, axis=1)], axis=0)
        far = moved(flat, order[...])
        out[component, 0] = far[:rows]
        out[component, 1] = far[rows:]


ALONE = pltpu.CompilerParams(vmem_limit_bytes=60 * 1024 * 1024)
SHARED = pltpu.CompilerParams(vmem_limit_bytes=24 * 1024 * 1024)


COST = pl.CostEstimate(flops=1 << 20, bytes_accessed=1 << 16, transcendentals=0)


LONG = pl.CostEstimate(flops=1 << 37, bytes_accessed=1 << 29, transcendentals=0)


def whole(kernel, shapes, *args, after=(), params=SHARED, cost=COST):
    shapes = [jax.ShapeDtypeStruct(shape, f32) for shape in shapes]
    in_vmem = pl.BlockSpec(memory_space=pltpu.VMEM)
    result = pl.pallas_call(
        kernel,
        out_shape=shapes,
        in_specs=[in_vmem] * len(args) + [pl.BlockSpec(memory_space=pl.ANY)] * len(after),
        out_specs=[in_vmem] * len(shapes),
        compiler_params=params,
        cost_estimate=cost,
    )(*args, *after)
    return result if len(shapes) > 1 else result[0]


def zero_kernel(*refs):
    refs[-1][...] = jnp.zeros(refs[-1].shape, f32)


def zeros_after(*arrays):
    return whole(zero_kernel, [(8, LANES)], after=arrays, cost=LONG)


def halves_kernel(both, *refs):
    first, second = refs[-2:]
    first[...] = both[:RADIX]
    second[...] = both[RADIX:]


def fixed(shape):
    return pl.BlockSpec(shape, lambda *_: (0,) * len(shape))


def project_x(place, currents, component, shards, tables, far_gradient=None, after=None):
    rows, columns = currents.shape[2:]
    tile = rows // 2
    t_hi, t_lo = tables["x"]
    args = [place, currents, tables["row_tw"], t_hi, t_lo]
    in_specs = [
        pl.BlockSpec((1, 2, tile, columns), lambda i, _: (component, 0, i, 0)),
        fixed((2 * RADIX, SPAN)),
        fixed(t_hi.shape),
        fixed(t_lo.shape),
    ]
    out_specs = [pl.BlockSpec((RADIX, tile, LANES), lambda i, _: (0, i, 0))] * shards
    shapes = [(RADIX, rows, LANES)] * shards
    if far_gradient is not None:
        args += [after, far_gradient, tables["order"]]
        in_specs += [pl.BlockSpec(memory_space=pl.ANY)]
        in_specs += [fixed(far_gradient.shape), fixed(tables["order"].shape)]
        shapes.insert(0, (2 * RADIX, far_gradient.shape[2], LANES))
        out_specs.insert(0, fixed(shapes[0]))
    return pl.pallas_call(
        functools.partial(x_kernel, shards),
        grid_spec=pltpu.PrefetchScalarGridSpec(
            num_scalar_prefetch=1,
            grid=(rows // tile,),
            in_specs=in_specs,
            out_specs=out_specs,
            scratch_shapes=[pltpu.VMEM((shards, RADIX, tile, LANES), f32)],
        ),
        out_shape=[jax.ShapeDtypeStruct(shape, f32) for shape in shapes],
        compiler_params=ALONE,
        cost_estimate=COST,
    )(*args)


def back_x(place, parts, component, grad, shape, tables):
    rows = shape[2]
    tile = rows // 2
    t_hi, t_lo = tables["x_back"]
    both = pl.BlockSpec((RADIX, tile, LANES), lambda i, _: (component, i, 0))
    one = pl.BlockSpec((RADIX, tile, LANES), lambda i, _: (0, i, 0))
    first = grad is None
    return pl.pallas_call(
        x_back_kernel,
        grid_spec=pltpu.PrefetchScalarGridSpec(
            num_scalar_prefetch=1,
            grid=(rows // tile,),
            in_specs=[pl.BlockSpec(memory_space=pl.ANY)]
            + [both if part.shape[0] > RADIX else one for part in parts]
            + [fixed((2 * RADIX, SPAN)), fixed(t_hi.shape), fixed(t_lo.shape)],
            out_specs=[
                pl.BlockSpec((1, 2, tile, shape[3]), lambda i, _: (component, 0, i, 0)),
                fixed((8, LANES)),
            ],
            scratch_shapes=[
                pltpu.VMEM((2 * RADIX * tile, 2 * BANDS), bf16),
                pltpu.VMEM((2 * RADIX * tile, 2 * BANDS), bf16),
            ],
        ),
        out_shape=[jax.ShapeDtypeStruct(shape, f32), jax.ShapeDtypeStruct((8, LANES), f32)],
        input_output_aliases={} if first else {1: 0},
        compiler_params=SHARED,
        cost_estimate=LONG if first else COST,
    )(place, tables["row_tw"] if first else grad, *parts, tables["row_tw"], t_hi, t_lo)


PAIRS = [(0, 1), (1, 0), (2, 3), (3, 2)]
SKIPS = [(0, 2), (2, 0), (1, 3), (3, 1)]


def send(value, pairs):
    return lax.ppermute(value, "narrow", pairs)


def fast_body(tables, currents, far_gradient):
    shards = lax.axis_size("narrow")
    wide = lax.axis_size("wide")
    rows = currents.shape[2]
    angle_rows = far_gradient.shape[2]
    scale = 1.0 / math.sqrt(rows * wide * NX)
    place = lax.axis_index("narrow").astype(jnp.int32).reshape(1)
    y_hi, y_lo = tables["y"]
    b_hi, b_lo = tables["y_back"]

    group = (RADIX, rows, LANES)
    blocks = [project_x(place, currents, 0, shards, tables)]
    far = [send(blocks[0][3], PAIRS)]
    sorted_, *rest = project_x(
        place, currents, 1, shards, tables, far_gradient, blocks[0][0]
    )
    blocks.append(rest)
    far.append(send(blocks[1][3], PAIRS))
    later = zeros_after(far[0])[0, 0]
    onward = jnp.concatenate([blocks[0][2] + far[0], blocks[1][2] + far[1]], axis=0)
    skip = send(onward, SKIPS)
    near = send(jnp.concatenate([blocks[c][1] + later for c in range(2)], axis=0), PAIRS)

    rows_in = lax.all_to_all(sorted_, "wide", 0, 0).reshape(MY, LANES)
    rows_out = whole(
        functools.partial(y_back_kernel, scale),
        [(rows * wide, LANES)],
        rows_in,
        tables["col_tw"],
        b_hi,
        b_lo,
        after=[onward],
    )
    half = lax.all_to_all(rows_out.reshape(wide, rows, LANES), "wide", 0, 0)
    beside = send(half, PAIRS)

    columns = jnp.concatenate([blocks[c][0] for c in range(2)], axis=0) + near + skip
    columns = columns + zeros_after(near)[0, 0]

    mine = whole(halves_kernel, [group, group], half, after=[columns])
    there = [send(m, SKIPS) for m in mine]

    rows_in = lax.all_to_all(columns, "wide", 0, 0).reshape(rows * wide, LANES)
    rows_out = whole(
        functools.partial(y_kernel, scale),
        [(MY, LANES)],
        rows_in,
        tables["col_tw"],
        y_hi,
        y_lo,
        after=[zeros_after(there[0], beside)],
    )
    far = lax.all_to_all(rows_out.reshape(wide, angle_rows, LANES), "wide", 0, 0)

    across = [send(t, PAIRS) for t in there]
    grad, _ = back_x(place, [mine[0], beside, there[0], across[0]], 0, None, currents.shape, tables)
    far_field = whole(unsort_kernel, [far_gradient.shape], far, tables["order_back"])
    grad, _ = back_x(place, [mine[1], beside, there[1], across[1]], 1, grad, currents.shape, tables)
    return (far_field, grad)


def solution(mesh):
    spec = P(None, None, "wide", "narrow")
    shards, wide = mesh.shape["narrow"], mesh.shape["wide"]

    def run(currents, far_gradient):
        rows = currents.shape[2]
        fits = (
            shards == 4
            and currents.shape[3] == shards * PERIOD
            and rows == 2 * SPAN
            and far_gradient.shape[2] == MY == 2 * SPAN
            and BANDS // shards == HALF
            and wide == 2 * RADIX
        )
        body = functools.partial(fast_body, make_tables(shards)) if fits else general_body
        return jax.shard_map(
            body, mesh=mesh, in_specs=(spec, spec), out_specs=(spec, spec), check_vma=False
        )(currents, far_gradient)

    return run
```
